32 devices in a mesh: mode: 4 (over y, x), mesh: 8 (over z, core).
Axes of the slice: x: 2, y: 2, z: 4, core: 2. Of those that a mesh axis runs over, the one named last changes fastest.
Arguments:
- b_field: float32 [128, 2, 3, 16384], P('mode', None, None, 'mesh'), may hold values from -6 to 6
- nu_coef: float32 [2, 17, 16384], P(None, None, 'mesh'), may hold values from -4 to 4
- nu_modes: int32 [17], replicated, may hold values from 0 to 127, as said below
- inv_mass: float32 [16384], P('mesh'), may hold values from 0.5 to 2
- connect: int32 [6, 8192], P(None, 'mesh'), may hold values from 0 to 2047
- stiff_plane: float32 [6, 6, 8192], P(None, None, 'mesh'), as said below
- stiff_mode: float32 [6, 6, 8192], P(None, None, 'mesh'), as said below
- shared_nodes: int32 [8, 2, 128], P('mesh'), may hold values from 0 to 2047, as said below
Outputs:
- b_next: float32 [128, 2, 3, 16384], P('mode', None, None, 'mesh')
The draws below stay inside these ranges and needn't reach their ends.
Inputs may be any that keep to these rules, and one draw needn't show every extreme that they name: `nu_modes`: the 17 mode numbers are distinct. `shared_nodes`: in each partition the 256 entries are distinct local nodes. `stiff_plane`: each element matrix is symmetric. `stiff_mode`: each element matrix is symmetric.
All inputs are finite; a program needn't handle non-finite values.
Results may differ from the reference program's by a relative error of at most 0.000075.
Values sent between devices are 32-bit elements; how exact they have to be, the bound alone decides.
A program may use at most 128 MiB of HBM per device.

```python
import math
import jax
import jax.numpy as jnp
from jax import lax

M = 128
NU_TERMS = 17
NLOC = 2048
ELEM_DEV = 1024
SHARED = 128
NODES = 16384
ELEMS = 8192
N_MESH = 8


def element_matrices(key, factor):
    key_off, key_diag = jax.random.split(key)
    off = jax.random.uniform(key_off, (6, 6, ELEMS), jnp.float32, -0.4, 0.4)
    off = 0.5 * (off + jnp.transpose(off, (1, 0, 2)))
    diag = jax.random.uniform(key_diag, (6, ELEMS), jnp.float32, 1.0, 2.0)
    ident = jnp.eye(6, dtype=jnp.float32)[:, :, None]
    return factor * (off * (1.0 - ident) + ident * diag[None, :, :])


def draw_stiff_plane(key, part):
    key = jax.random.fold_in(key, 1)
    return element_matrices(key, 1.0)


def draw_stiff_mode(key, part):
    key = jax.random.fold_in(key, 2)
    return element_matrices(key, 0.00025)


def draw_nu_modes(key, part):
    key = jax.random.fold_in(key, 3)
    others = jax.random.permutation(key, M - 2)[:NU_TERMS - 2].astype(jnp.int32) + 1
    ends = jnp.array([0, M - 1], dtype=jnp.int32)
    return jnp.concatenate([ends, others]).astype(jnp.int32)


def draw_shared_nodes(key, part):
    key = jax.random.fold_in(key, 4)
    keys = jax.random.split(key, N_MESH)
    perms = jax.vmap(lambda k: jax.random.permutation(k, NLOC))(keys)
    return perms[:, :2 * SHARED].reshape(N_MESH, 2, SHARED).astype(jnp.int32)


def plant(entries, stream_key, low, high):
    extent = entries.shape
    place = [jax.random.randint(jax.random.fold_in(stream_key, axis), (), 0, extent[axis]) for axis in range(len(extent))]
    entries = entries.at[tuple(place)].set(low)
    longest = extent.index(max(extent))
    place[longest] = (place[longest] + 1) % extent[longest]
    return entries.at[tuple(place)].set(high)


def block_scale(rng, extent, pieces, least, high):
    factor_of = 1.0
    for dim, blocks in pieces:
        steps = jax.random.uniform(jax.random.fold_in(jax.random.fold_in(rng, 6), dim), (blocks,), jnp.float32, least / len(pieces), high / len(pieces))
        factor_of = factor_of * jnp.repeat(jnp.exp(steps), extent[dim] // blocks).reshape((-1,) + (1,) * (len(extent) - 1 - dim))
    return factor_of


def gaussian(own_key, dims, deviation, reach, cuts=(), kind=jnp.bfloat16):
    values = deviation * jax.random.normal(own_key, dims, jnp.float32)
    if cuts:
        values = values * block_scale(own_key, dims, cuts, -0.22, 0.18)
    return jnp.clip(values, -reach, reach).astype(kind)


def setup_inputs(seed: int = 0) -> dict:
    seeds = jax.random.split(jax.random.key(seed), 9)
    return {
        "b_field": gaussian(seeds[0], (M, 2, 3, NODES), 1.0, 6.0, ((0, 4), (3, 8)), jnp.float32),
        "nu_coef": gaussian(seeds[1], (2, NU_TERMS, NODES), 0.3, 4.0, ((2, 8),), jnp.float32),
        "nu_modes": draw_nu_modes(jax.random.fold_in(seeds[8], 71), 0),
        "inv_mass": jnp.clip(jnp.exp(math.log(2.0) - 1.3862944 * jax.random.uniform(seeds[3], (NODES,), jnp.float32) ** block_scale(seeds[3], (NODES,), ((0, 8),), -0.2, 0.2)), 0.5, 2.0),
        "connect": plant(jax.random.randint(seeds[4], (6, ELEMS), 0, NLOC), jax.random.fold_in(seeds[4], 1), 0, NLOC - 1).astype(jnp.int32),
        "stiff_plane": draw_stiff_plane(jax.random.fold_in(seeds[8], 71), 0),
        "stiff_mode": draw_stiff_mode(jax.random.fold_in(seeds[8], 71), 0),
        "shared_nodes": draw_shared_nodes(jax.random.fold_in(seeds[8], 71), 0),
    }


time_step = 0.1


def couple(field, nu_coef, nu_modes):
    result = jnp.zeros_like(field)
    for j in range(NU_TERMS):
        rolled = jnp.roll(field, nu_modes[j], axis=0)
        real_part = nu_coef[0, j] * rolled[:, 0] - nu_coef[1, j] * rolled[:, 1]
        imag_part = nu_coef[0, j] * rolled[:, 1] + nu_coef[1, j] * rolled[:, 0]
        result = result + jnp.stack([real_part, imag_part], axis=1)
    return result


def rate(field, nu_coef, nu_modes, inv_mass, connect, stiff_plane, stiff_mode, shared_nodes):
    coupled = couple(field, nu_coef, nu_modes)
    owner = (jnp.arange(ELEMS, dtype=jnp.int32) // ELEM_DEV) * NLOC
    global_idx = connect + owner[None, :]
    modes = jnp.arange(M, dtype=jnp.int32)
    mode_abs = jnp.minimum(modes, M - modes).astype(jnp.float32)
    lower = shared_nodes[:, 0]
    upper = shared_nodes[:, 1]
    parts = jnp.arange(N_MESH, dtype=jnp.int32)[:, None]

    def one_mode(args):
        values, weight = args
        flat = values.reshape(6, NODES)
        picked = flat[:, global_idx]
        plane = jnp.einsum('bae,cae->cbe', stiff_plane, picked, precision=lax.Precision.HIGHEST)
        extra = jnp.einsum('bae,cae->cbe', stiff_mode, picked, precision=lax.Precision.HIGHEST)
        terms = plane + (weight * weight) * extra
        summed = jnp.zeros((6, NODES), jnp.float32).at[:, global_idx].add(terms)
        blocks = summed.reshape(6, N_MESH, NLOC)
        sent_up = blocks[:, parts, upper]
        sent_low = blocks[:, parts, lower]
        zero_row = jnp.zeros((6, 1, SHARED), jnp.float32)
        below = jnp.concatenate([zero_row, sent_up[:, :-1]], axis=1)
        above = jnp.concatenate([sent_low[:, 1:], zero_row], axis=1)
        blocks = blocks.at[:, parts, lower].add(below)
        blocks = blocks.at[:, parts, upper].add(above)
        return blocks.reshape(2, 3, NODES)

    assembled = lax.map(one_mode, (coupled, mode_abs))
    return -inv_mass * assembled


def reference(b_field, nu_coef, nu_modes, inv_mass, connect, stiff_plane, stiff_mode, shared_nodes):
    rest = (nu_coef, nu_modes, inv_mass, connect, stiff_plane, stiff_mode, shared_nodes)
    b_mid = b_field + time_step * rate(b_field, *rest)
    return 0.5 * b_field + 0.5 * (b_mid + time_step * rate(b_mid, *rest))
```

```python
import functools
import jax
import jax.numpy as jnp
from jax import lax
from jax.experimental import pallas as pl
from jax.experimental.pallas import tpu as pltpu
from jax.sharding import PartitionSpec as P

time_step = 0.1
f32, bf16 = jnp.float32, jnp.bfloat16
lanes = 128
tile = 256


def from_behind(block, axis, distance):
    devices = range(lax.axis_size(axis))
    route = [(i - distance, i) for i in devices if i - distance in devices]
    return lax.ppermute(block, axis, route)


def halves(value):
    high = value.astype(bf16)
    return high, (value - high.astype(f32)).astype(bf16)


def lane_slice(index, width):
    return pl.ds(pl.multiple_of(index * width, width), width)


def fill_select(shared_ref, select_ref):
    nloc = select_ref.shape[0]
    ids = lax.broadcasted_iota(jnp.int32, (nloc, lanes), 0)
    for side in range(2):
        hit = ids == shared_ref[side : side + 1, :]
        select_ref[:, side * lanes : (side + 1) * lanes] = jnp.where(hit, 1.0, 0.0).astype(bf16)


def received_at(got_ref, split_ref, select_ref, cols):
    rows = got_ref.shape[1]
    both = lax.dot_general(
        split_ref[...], select_ref[cols, :], (((1,), (1,)), ((), ())), preferred_element_type=f32
    )
    return both[:rows] + both[rows:]


def split_received(got_ref, split_ref):
    rows = got_ref.shape[1]
    for side in range(2):
        high, low = halves(got_ref[side])
        split_ref[:rows, side * lanes : (side + 1) * lanes] = high
        split_ref[rows:, side * lanes : (side + 1) * lanes] = low


def couple(x_ref, coef_ref, nu_modes_ref, h_ref):
    pieces, total = x_ref.shape[1], x_ref.shape[2] // 2
    rows = 2 * total
    step = 64

    @pl.loop(0, pieces)
    def _(nt):
        cols = lane_slice(nt, lanes)
        for start in range(0, total, step):
            re = jnp.zeros((step, lanes), f32)
            im = jnp.zeros((step, lanes), f32)
            for j in range(coef_ref.shape[1]):
                begin = total + start - nu_modes_ref[j]
                xr = x_ref[0, nt, pl.ds(begin, step), :]
                xi = x_ref[1, nt, pl.ds(begin, step), :]
                cr = coef_ref[0, j : j + 1, cols]
                ci = coef_ref[1, j : j + 1, cols]
                re = re + (cr * xr - ci * xi)
                im = im + (cr * xi + ci * xr)
            for part, value in ((0, re), (1, im)):
                high, low = halves(value)
                base = part * total + start
                h_ref[base : base + step, cols] = high
                h_ref[rows + base : rows + base + step, cols] = low


def stiffness(h_ref, connect_ref, plane_ref, mode_ref, t_ref, p_ref, y_ref, z_ref):
    rows, nloc = z_ref.shape
    total = rows // 2
    elems = connect_ref.shape[1]
    z_ref[...] = jnp.zeros_like(z_ref)
    chunk = 256
    band = 16

    @pl.loop(0, elems // tile)
    def _(t):
        @pl.loop(0, nloc // chunk)
        def _(n):
            ids = lax.broadcasted_iota(jnp.int32, (chunk, tile), 0) + n * chunk
            for a in range(6):
                hit = ids == connect_ref[a : a + 1, lane_slice(t, tile)]
                t_ref[lane_slice(n, chunk), a * tile : (a + 1) * tile] = jnp.where(
                    hit, 1.0, 0.0
                ).astype(bf16)

        @pl.loop(0, 6)
        def _(a):
            both = jnp.dot(h_ref[...], t_ref[:, lane_slice(a, tile)], preferred_element_type=f32)
            p_ref[a] = both[:rows] + both[rows:]

        @pl.loop(0, total // band)
        def _(g):
            at = pl.multiple_of(g * band, band)
            m = lax.broadcasted_iota(jnp.int32, (band, lanes), 0) + at
            mm = jnp.minimum(m, total - m).astype(f32)
            weight = mm * mm
            for piece in range(tile // lanes):
                cols = pl.ds(pl.multiple_of(t * tile + piece * lanes, lanes), lanes)
                near = slice(piece * lanes, (piece + 1) * lanes)
                picked = [
                    [p_ref[a, pl.ds(part * total + at, band), near] for a in range(6)]
                    for part in range(2)
                ]
                y = [[jnp.zeros((band, lanes), f32)] * 6 for part in range(2)]
                for b in range(6):
                    for a in range(b, 6):
                        s = plane_ref[b, a : a + 1, cols] + weight * mode_ref[b, a : a + 1, cols]
                        for part in range(2):
                            y[part][b] = y[part][b] + s * picked[part][a]
                            if a != b:
                                y[part][a] = y[part][a] + s * picked[part][b]
                for part in range(2):
                    for b in range(6):
                        high, low = halves(y[part][b])
                        here = slice(b * tile + piece * lanes, b * tile + (piece + 1) * lanes)
                        base = part * total + at
                        y_ref[pl.ds(pl.multiple_of(base, band), band), here] = high
                        y_ref[pl.ds(pl.multiple_of(rows + base, band), band), here] = low

        @pl.loop(0, nloc // chunk)
        def _(n):
            cols = lane_slice(n, chunk)
            both = lax.dot_general(
                y_ref[...],
                t_ref[cols, :],
                (((1,), (1,)), ((), ())),
                preferred_element_type=f32,
            )
            z_ref[:, cols] += both[:rows] + both[rows:]


def send_values(z_ref, h_ref, select_ref, sent_ref):
    rows = z_ref.shape[0]

    @pl.loop(0, z_ref.shape[1] // 256)
    def _(n):
        cols = lane_slice(n, 256)
        high, low = halves(z_ref[:, cols])
        h_ref[:rows, cols] = high
        h_ref[rows:, cols] = low

    both = jnp.dot(h_ref[...], select_ref[...], preferred_element_type=f32)
    both = both[:rows] + both[rows:]
    sent_ref[0] = both[:, :lanes]
    sent_ref[1] = both[:, lanes:]


def put_field(x_ref, part, nt, start, value):
    total = x_ref.shape[2] // 2
    count = value.shape[0]
    x_ref[part, nt, start : start + count, :] = value
    x_ref[part, nt, total + start : total + start + count, :] = value


def first_kernel(
    nu_modes_ref, b_ref, coef_ref, connect_ref, plane_ref, mode_ref, shared_ref,
    z_ref, sent_ref, x_ref, h_ref, t_ref, p_ref, y_ref, select_ref,
):
    sources, _, count, nloc = b_ref.shape
    fill_select(shared_ref, select_ref)

    @pl.loop(0, nloc // lanes)
    def _(nt):
        for source in range(sources):
            for part in range(2):
                put_field(x_ref, part, nt, source * count, b_ref[source, part, :, lane_slice(nt, lanes)])

    couple(x_ref, coef_ref, nu_modes_ref, h_ref)
    stiffness(h_ref, connect_ref, plane_ref, mode_ref, t_ref, p_ref, y_ref, z_ref)
    send_values(z_ref, h_ref, select_ref, sent_ref)


def second_kernel(
    nu_modes_ref, b_ref, coef_ref, connect_ref, plane_ref, mode_ref, shared_ref,
    inv_ref, z1_ref, got_ref,
    z_ref, sent_ref, mid_ref, x_ref, h_ref, t_ref, p_ref, y_ref, select_ref, split_ref,
):
    sources, _, count, nloc = b_ref.shape
    total = sources * count
    fill_select(shared_ref, select_ref)
    split_received(got_ref, split_ref)

    @pl.loop(0, nloc // tile)
    def _(n):
        added = received_at(got_ref, split_ref, select_ref, lane_slice(n, tile))
        for piece in range(tile // lanes):
            nt = n * (tile // lanes) + piece
            cols = lane_slice(nt, lanes)
            drop = -time_step * inv_ref[:, cols]
            for source in range(sources):
                for part in range(2):
                    base = part * total + source * count
                    s = z1_ref[base : base + count, cols]
                    s = s + added[base : base + count, piece * lanes : (piece + 1) * lanes]
                    value = b_ref[source, part, :, cols] + drop * s
                    mid_ref[source, part, :, cols] = value
                    put_field(x_ref, part, nt, source * count, value)

    couple(x_ref, coef_ref, nu_modes_ref, h_ref)
    stiffness(h_ref, connect_ref, plane_ref, mode_ref, t_ref, p_ref, y_ref, z_ref)
    send_values(z_ref, h_ref, select_ref, sent_ref)


def last_kernel(
    b_ref, mid_ref, shared_ref, inv_ref, z_ref, got_ref, out_ref, select_ref, split_ref
):
    sources, _, count, nloc = b_ref.shape
    total = sources * count
    fill_select(shared_ref, select_ref)
    split_received(got_ref, split_ref)

    @pl.loop(0, nloc // tile)
    def _(n):
        cols = lane_slice(n, tile)
        added = received_at(got_ref, split_ref, select_ref, cols)
        drop = -time_step * inv_ref[:, cols]
        for source in range(sources):
            for part in range(2):
                base = part * total + source * count
                s = z_ref[base : base + count, cols] + added[base : base + count]
                value = mid_ref[source, part, :, cols] + drop * s
                out_ref[source, part, :, cols] = 0.5 * b_ref[source, part, :, cols] + 0.5 * value


def exchange(sent):
    below = from_behind(sent[1], "mesh", 1)
    above = from_behind(sent[0], "mesh", -1)
    return jnp.stack([below, above])


def body(b_field, nu_coef, nu_modes, inv_mass, connect, stiff_plane, stiff_mode, shared_nodes):
    count, _, comps, nloc = b_field.shape
    sources = lax.axis_size("mode")
    total = sources * count
    rows = 2 * total
    parts = jnp.transpose(b_field, (2, 1, 0, 3))
    parts = jnp.pad(parts, ((0, sources - comps), (0, 0), (0, 0), (0, 0)))
    mine = lax.all_to_all(parts, "mode", 0, 0, tiled=True)
    inv = inv_mass[None, :]
    shared = shared_nodes[0]
    vmem = pl.BlockSpec(memory_space=pltpu.VMEM)
    smem = pl.BlockSpec(memory_space=pltpu.SMEM)
    params = pltpu.CompilerParams(vmem_limit_bytes=56 * 1024 * 1024)
    scratch = [
        pltpu.VMEM((2, nloc // lanes, 2 * total, lanes), f32),
        pltpu.VMEM((2 * rows, nloc), bf16),
        pltpu.VMEM((nloc, 6 * tile), bf16),
        pltpu.VMEM((6, rows, tile), f32),
        pltpu.VMEM((2 * rows, 6 * tile), bf16),
        pltpu.VMEM((nloc, 2 * lanes), bf16),
    ]
    split = pltpu.VMEM((2 * rows, 2 * lanes), bf16)
    z_shape = jax.ShapeDtypeStruct((rows, nloc), f32)
    sent_shape = jax.ShapeDtypeStruct((2, rows, lanes), f32)
    field_shape = jax.ShapeDtypeStruct(mine.shape, f32)
    fixed = (nu_coef, connect, stiff_plane, stiff_mode, shared)
    z1, sent = pl.pallas_call(
        first_kernel, out_shape=(z_shape, sent_shape), in_specs=[smem] + [vmem] * 6,
        out_specs=(vmem, vmem), scratch_shapes=scratch, compiler_params=params,
    )(nu_modes, mine, *fixed)
    z2, sent2, mid = pl.pallas_call(
        second_kernel, out_shape=(z_shape, sent_shape, field_shape), in_specs=[smem] + [vmem] * 9,
        out_specs=(vmem, vmem, vmem), scratch_shapes=scratch + [split], compiler_params=params,
    )(nu_modes, mine, *fixed, inv, z1, exchange(sent))
    done = pl.pallas_call(
        last_kernel, out_shape=field_shape, in_specs=[vmem] * 6, out_specs=vmem,
        scratch_shapes=[scratch[-1], split], compiler_params=params,
    )(mine, mid, shared, inv, z2, exchange(sent2))
    back = lax.all_to_all(done, "mode", 0, 0, tiled=True)
    return jnp.transpose(back[:comps], (2, 1, 0, 3))


def solution(mesh):
    placed = (
        P("mode", None, None, "mesh"),
        P(None, None, "mesh"),
        P(),
        P("mesh"),
        P(None, "mesh"),
        P(None, None, "mesh"),
        P(None, None, "mesh"),
        P("mesh", None, None),
    )
    return jax.shard_map(
        body, mesh=mesh, in_specs=placed, out_specs=P("mode", None, None, "mesh"), check_vma=False
    )
```

```python
import functools
import jax
import jax.numpy as jnp
from jax import lax
from jax.experimental import pallas as pl
from jax.experimental.pallas import tpu as pltpu
from jax.sharding import PartitionSpec as P

time_step = 0.1
f32, bf16 = jnp.float32, jnp.bfloat16
lanes = 128
tile = 256


def from_behind(block, axis, distance):
    devices = range(lax.axis_size(axis))
    route = [(i - distance, i) for i in devices if i - distance in devices]
    return lax.ppermute(block, axis, route)


def halves(value):
    high = value.astype(bf16)
    return high, (value - high.astype(f32)).astype(bf16)


def lane_slice(index, width):
    return pl.ds(pl.multiple_of(index * width, width), width)


def fill_select(shared_ref, select_ref):
    nloc = select_ref.shape[0]
    ids = lax.broadcasted_iota(jnp.int32, (nloc, lanes), 0)
    for side in range(2):
        hit = ids == shared_ref[side : side + 1, :]
        select_ref[:, side * lanes : (side + 1) * lanes] = jnp.where(hit, 1.0, 0.0).astype(bf16)


def received_at(got_ref, split_ref, select_ref, cols):
    rows = got_ref.shape[1]
    both = lax.dot_general(
        split_ref[...], select_ref[cols, :], (((1,), (1,)), ((), ())), preferred_element_type=f32
    )
    return both[:rows] + both[rows:]


def split_received(got_ref, split_ref):
    rows = got_ref.shape[1]
    for side in range(2):
        high, low = halves(got_ref[side])
        split_ref[:rows, side * lanes : (side + 1) * lanes] = high
        split_ref[rows:, side * lanes : (side + 1) * lanes] = low


def couple(x_ref, coef_ref, nu_modes_ref, h_ref):
    pieces, total = x_ref.shape[1], x_ref.shape[2] // 2
    rows = 2 * total
    step = 32

    @pl.loop(0, pieces)
    def _(nt):
        cols = lane_slice(nt, lanes)
        for start in range(0, total, step):
            re = jnp.zeros((step, lanes), f32)
            im = jnp.zeros((step, lanes), f32)
            for j in range(coef_ref.shape[1]):
                begin = total + start - nu_modes_ref[j]
                xr = x_ref[0, nt, pl.ds(begin, step), :]
                xi = x_ref[1, nt, pl.ds(begin, step), :]
                cr = coef_ref[0, j : j + 1, cols]
                ci = coef_ref[1, j : j + 1, cols]
                re = re + (cr * xr - ci * xi)
                im = im + (cr * xi + ci * xr)
            for part, value in ((0, re), (1, im)):
                high, low = halves(value)
                base = part * total + start
                h_ref[base : base + step, cols] = high
                h_ref[rows + base : rows + base + step, cols] = low


def one_hot(hit):
    return jnp.where(hit, 1.0, 0.0).astype(bf16)


def gather(h_ref, connect_ref, p_ref, t):
    rows, nloc = h_ref.shape[0] // 2, h_ref.shape[1]

    @pl.loop(0, 6)
    def _(a):
        ids = lax.broadcasted_iota(jnp.int32, (nloc, tile), 0)
        table = one_hot(ids == connect_ref[pl.ds(a, 1), lane_slice(t, tile)])
        both = jnp.dot(h_ref[...], table, preferred_element_type=f32)
        p_ref[a] = both[:rows] + both[rows:]


def elements(plane_ref, mode_ref, p_ref, y_ref, t):
    rows = y_ref.shape[0] // 2
    total = rows // 2
    band = 16

    @pl.loop(0, total // band)
    def _(g):
        at = pl.multiple_of(g * band, band)
        m = lax.broadcasted_iota(jnp.int32, (band, lanes), 0) + at
        mm = jnp.minimum(m, total - m).astype(f32)
        weight = mm * mm
        for piece in range(tile // lanes):
            cols = pl.ds(pl.multiple_of(t * tile + piece * lanes, lanes), lanes)
            near = slice(piece * lanes, (piece + 1) * lanes)
            picked = [
                [p_ref[a, pl.ds(part * total + at, band), near] for a in range(6)]
                for part in range(2)
            ]
            y = [[jnp.zeros((band, lanes), f32)] * 6 for part in range(2)]
            for b in range(6):
                for a in range(b, 6):
                    s = plane_ref[b, a : a + 1, cols] + weight * mode_ref[b, a : a + 1, cols]
                    for part in range(2):
                        y[part][b] = y[part][b] + s * picked[part][a]
                        if a != b:
                            y[part][a] = y[part][a] + s * picked[part][b]
            for part in range(2):
                for b in range(6):
                    high, low = halves(y[part][b])
                    here = slice(b * tile + piece * lanes, b * tile + (piece + 1) * lanes)
                    base = part * total + at
                    y_ref[pl.ds(pl.multiple_of(base, band), band), here] = high
                    y_ref[pl.ds(pl.multiple_of(rows + base, band), band), here] = low


def scatter(y_ref, columns_ref, z_ref, t):
    rows, nloc = z_ref.shape
    chunk = 512

    @pl.loop(0, nloc // chunk)
    def _(n):
        cols = lane_slice(n, chunk)
        ids = lax.broadcasted_iota(jnp.int32, (tile, lanes), 1) + n * chunk
        slots = []
        for b in range(6):
            nodes = columns_ref[b, lane_slice(t, tile), :]
            pieces = [one_hot(ids + k * lanes == nodes) for k in range(chunk // lanes)]
            slots.append(jnp.concatenate(pieces, axis=1))
        table = jnp.concatenate(slots, axis=0)
        both = jnp.dot(y_ref[...], table, preferred_element_type=f32)
        z_ref[:, cols] += both[:rows] + both[rows:]


def stiffness(h_ref, connect_ref, plane_ref, mode_ref, turned_ref, p_ref, y_ref, columns_ref, z_ref):
    z_ref[...] = jnp.zeros_like(z_ref)
    elems = connect_ref.shape[1]
    for b in range(6):
        columns_ref[b] = jnp.broadcast_to(turned_ref[:, b : b + 1], (elems, lanes))

    @pl.loop(0, elems // tile)
    def _(t):
        gather(h_ref, connect_ref, p_ref, t)
        elements(plane_ref, mode_ref, p_ref, y_ref, t)
        scatter(y_ref, columns_ref, z_ref, t)


def send_values(z_ref, h_ref, select_ref, sent_ref):
    rows = z_ref.shape[0]

    @pl.loop(0, z_ref.shape[1] // 256)
    def _(n):
        cols = lane_slice(n, 256)
        high, low = halves(z_ref[:, cols])
        h_ref[:rows, cols] = high
        h_ref[rows:, cols] = low

    both = jnp.dot(h_ref[...], select_ref[...], preferred_element_type=f32)
    both = both[:rows] + both[rows:]
    sent_ref[0] = both[:, :lanes]
    sent_ref[1] = both[:, lanes:]


def put_field(x_ref, part, nt, start, value):
    total = x_ref.shape[2] // 2
    count = value.shape[0]
    x_ref[part, nt, start : start + count, :] = value
    x_ref[part, nt, total + start : total + start + count, :] = value


def first_kernel(
    nu_modes_ref, b_ref, coef_ref, connect_ref, turned_ref, plane_ref, mode_ref, shared_ref,
    z_ref, sent_ref, x_ref, h_ref, p_ref, y_ref, columns_ref, select_ref,
):
    sources, _, count, nloc = b_ref.shape
    fill_select(shared_ref, select_ref)

    @pl.loop(0, nloc // lanes)
    def _(nt):
        for source in range(sources):
            for part in range(2):
                put_field(x_ref, part, nt, source * count, b_ref[source, part, :, lane_slice(nt, lanes)])

    couple(x_ref, coef_ref, nu_modes_ref, h_ref)
    stiffness(h_ref, connect_ref, plane_ref, mode_ref, turned_ref, p_ref, y_ref, columns_ref, z_ref)
    send_values(z_ref, h_ref, select_ref, sent_ref)


def second_kernel(
    nu_modes_ref, b_ref, coef_ref, connect_ref, turned_ref, plane_ref, mode_ref, shared_ref,
    inv_ref, z1_ref, got_ref,
    z_ref, sent_ref, mid_ref, x_ref, h_ref, p_ref, y_ref, columns_ref, select_ref, split_ref,
):
    sources, _, count, nloc = b_ref.shape
    total = sources * count
    fill_select(shared_ref, select_ref)
    split_received(got_ref, split_ref)

    @pl.loop(0, nloc // tile)
    def _(n):
        added = received_at(got_ref, split_ref, select_ref, lane_slice(n, tile))
        for piece in range(tile // lanes):
            nt = n * (tile // lanes) + piece
            cols = lane_slice(nt, lanes)
            drop = -time_step * inv_ref[:, cols]
            for source in range(sources):
                for part in range(2):
                    base = part * total + source * count
                    s = z1_ref[base : base + count, cols]
                    s = s + added[base : base + count, piece * lanes : (piece + 1) * lanes]
                    value = b_ref[source, part, :, cols] + drop * s
                    mid_ref[source, part, :, cols] = value
                    put_field(x_ref, part, nt, source * count, value)

    couple(x_ref, coef_ref, nu_modes_ref, h_ref)
    stiffness(h_ref, connect_ref, plane_ref, mode_ref, turned_ref, p_ref, y_ref, columns_ref, z_ref)
    send_values(z_ref, h_ref, select_ref, sent_ref)


def last_kernel(
    b_ref, mid_ref, shared_ref, inv_ref, z_ref, got_ref, out_ref, select_ref, split_ref
):
    sources, _, count, nloc = b_ref.shape
    total = sources * count
    fill_select(shared_ref, select_ref)
    split_received(got_ref, split_ref)

    @pl.loop(0, nloc // tile)
    def _(n):
        cols = lane_slice(n, tile)
        added = received_at(got_ref, split_ref, select_ref, cols)
        drop = -time_step * inv_ref[:, cols]
        for source in range(sources):
            for part in range(2):
                base = part * total + source * count
                s = z_ref[base : base + count, cols] + added[base : base + count]
                value = mid_ref[source, part, :, cols] + drop * s
                out_ref[source, part, :, cols] = 0.5 * b_ref[source, part, :, cols] + 0.5 * value


def greet(devices):
    me = lax.axis_index("mode")
    barrier = pltpu.get_barrier_semaphore()
    for k in range(1, devices):
        pl.semaphore_signal(
            barrier, inc=1, device_id={"mode": (me + k) % devices}, device_id_type=pl.DeviceIdType.MESH
        )
    pl.semaphore_wait(barrier, devices - 1)
    return me


def remote(source_ref, target_ref, send_sem, recv_sem, k, device):
    return pltpu.make_async_remote_copy(
        src_ref=source_ref, dst_ref=target_ref, send_sem=send_sem.at[k], recv_sem=recv_sem.at[k],
        device_id={"mode": device}, device_id_type=pl.DeviceIdType.MESH,
    )


def spread_kernel(devices, comps, parts_ref, out_ref, send_sem, recv_sem, own_sem):
    me = greet(devices)

    def to(k):
        other = (me + k) % devices
        return other, other < comps

    for k in range(1, devices):
        other, wanted = to(k)

        @pl.when(wanted)
        def _():
            remote(parts_ref.at[other], out_ref.at[me], send_sem, recv_sem, k, other).start()

    @pl.when(me < comps)
    def _():
        own = pltpu.make_async_copy(parts_ref.at[me], out_ref.at[me], own_sem)
        own.start()
        own.wait()
        for k in range(1, devices):
            source = (me + devices - k) % devices
            remote(out_ref.at[source], out_ref.at[source], send_sem, recv_sem, k, source).wait_recv()

    for k in range(1, devices):
        other, wanted = to(k)

        @pl.when(wanted)
        def _():
            remote(parts_ref.at[other], out_ref.at[me], send_sem, recv_sem, k, other).wait_send()


def collect_kernel(devices, comps, done_ref, out_ref, send_sem, recv_sem, own_sem):
    me = greet(devices)

    @pl.when(me < comps)
    def _():
        for k in range(1, devices):
            other = (me + k) % devices
            remote(done_ref.at[other], out_ref.at[me], send_sem, recv_sem, k, other).start()
        own = pltpu.make_async_copy(done_ref.at[me], out_ref.at[me], own_sem)
        own.start()
        own.wait()

    for k in range(1, devices):
        source = (me + devices - k) % devices

        @pl.when(source < comps)
        def _():
            remote(out_ref.at[source], out_ref.at[source], send_sem, recv_sem, k, source).wait_recv()

    @pl.when(me < comps)
    def _():
        for k in range(1, devices):
            other = (me + k) % devices
            remote(done_ref.at[other], out_ref.at[me], send_sem, recv_sem, k, other).wait_send()


def move(kernel, block, devices, comps, out_blocks, name):
    where = pl.BlockSpec(memory_space=pl.ANY)
    return pl.pallas_call(
        functools.partial(kernel, devices, comps),
        out_shape=jax.ShapeDtypeStruct((out_blocks,) + block.shape[1:], f32),
        in_specs=[where], out_specs=where,
        scratch_shapes=[
            pltpu.SemaphoreType.DMA((devices,)),
            pltpu.SemaphoreType.DMA((devices,)),
            pltpu.SemaphoreType.DMA,
        ],
        compiler_params=pltpu.CompilerParams(collective_id=name, has_side_effects=True),
    )(block)


def exchange(sent):
    below = from_behind(sent[1], "mesh", 1)
    above = from_behind(sent[0], "mesh", -1)
    return jnp.stack([below, above])


def body(b_field, nu_coef, nu_modes, inv_mass, connect, stiff_plane, stiff_mode, shared_nodes):
    count, _, comps, nloc = b_field.shape
    sources = lax.axis_size("mode")
    total = sources * count
    rows = 2 * total
    parts = jnp.transpose(b_field, (2, 1, 0, 3))
    mine = move(spread_kernel, parts, sources, comps, sources, 0)
    inv = inv_mass[None, :]
    shared = shared_nodes[0]
    vmem = pl.BlockSpec(memory_space=pltpu.VMEM)
    smem = pl.BlockSpec(memory_space=pltpu.SMEM)
    params = pltpu.CompilerParams(vmem_limit_bytes=56 * 1024 * 1024)
    scratch = [
        pltpu.VMEM((2, nloc // lanes, 2 * total, lanes), f32),
        pltpu.VMEM((2 * rows, nloc), bf16),
        pltpu.VMEM((6, rows, tile), f32),
        pltpu.VMEM((2 * rows, 6 * tile), bf16),
        pltpu.VMEM((6, connect.shape[1], lanes), jnp.int32),
        pltpu.VMEM((nloc, 2 * lanes), bf16),
    ]
    split = pltpu.VMEM((2 * rows, 2 * lanes), bf16)
    z_shape = jax.ShapeDtypeStruct((rows, nloc), f32)
    sent_shape = jax.ShapeDtypeStruct((2, rows, lanes), f32)
    field_shape = jax.ShapeDtypeStruct(mine.shape, f32)
    fixed = (nu_coef, connect, connect.T, stiff_plane, stiff_mode, shared)
    z1, sent = pl.pallas_call(
        first_kernel, out_shape=(z_shape, sent_shape), in_specs=[smem] + [vmem] * 7,
        out_specs=(vmem, vmem), scratch_shapes=scratch, compiler_params=params,
    )(nu_modes, mine, *fixed)
    z2, sent2, mid = pl.pallas_call(
        second_kernel, out_shape=(z_shape, sent_shape, field_shape), in_specs=[smem] + [vmem] * 10,
        out_specs=(vmem, vmem, vmem), scratch_shapes=scratch + [split], compiler_params=params,
    )(nu_modes, mine, *fixed, inv, z1, exchange(sent))
    done = pl.pallas_call(
        last_kernel, out_shape=field_shape, in_specs=[vmem] * 6, out_specs=vmem,
        scratch_shapes=[scratch[-1], split], compiler_params=params,
    )(mine, mid, shared, inv, z2, exchange(sent2))
    back = move(collect_kernel, done, sources, comps, comps, 1)
    return jnp.transpose(back, (2, 1, 0, 3))


def solution(mesh):
    placed = (
        P("mode", None, None, "mesh"),
        P(None, None, "mesh"),
        P(),
        P("mesh"),
        P(None, "mesh"),
        P(None, None, "mesh"),
        P(None, None, "mesh"),
        P("mesh", None, None),
    )
    return jax.shard_map(
        body, mesh=mesh, in_specs=placed, out_specs=P("mode", None, None, "mesh"), check_vma=False
    )
```
